32 devices in a mesh: wide: 16 (over z, x, core), narrow: 2 (over y).
Axes of the slice: x: 2, y: 2, z: 4, core: 2. Of those that a mesh axis runs over, the one named last changes fastest.
Arguments:
- tokens: bfloat16 [12288, 2048], P(('wide', 'narrow')), may hold values from -6 to 6
- segment_ids: int32 [32, 384], P(('wide', 'narrow')), may hold values from 0 to 5, never falling along the last dimension, each value on 1 to 192 neighbouring positions
- language_ids: int32 [32, 384], P(('wide', 'narrow')), may hold values from 0 to 6
- lang_table: bfloat16 [2048, 7], P(('wide', 'narrow')), may hold values from -3 to 3
- norm1_gain: bfloat16 [2048], P(('wide', 'narrow')), may hold values from 0.5 to 1.5
- norm1_bias: bfloat16 [2048], P(('wide', 'narrow')), may hold values from -1 to 1
- qkv_weight: bfloat16 [6144, 2048], P(('wide', 'narrow')), may hold values from -0.125 to 0.125
- qkv_bias: bfloat16 [6144], P(('wide', 'narrow')), may hold values from -1.5 to 1.5
- out_weight: bfloat16 [2048, 2048], P(('wide', 'narrow')), may hold values from -0.75 to 0.75
- norm2_gain: bfloat16 [2048], P(('wide', 'narrow')), may hold values from 0.5 to 1.5
- norm2_bias: bfloat16 [2048], P(('wide', 'narrow')), may hold values from -1 to 1
- gate_up_weight: bfloat16 [11264, 2048], P(('wide', 'narrow')), may hold values from -0.125 to 0.125
- down_weight: bfloat16 [2048, 5632], P(('wide', 'narrow')), may hold values from -0.078125 to 0.078125
- cotangent: bfloat16 [12288, 2048], P(('wide', 'narrow')), may hold values from -6 to 6
Outputs:
- mixed: bfloat16 [12288, 2048], P(('wide', 'narrow'))
- token_grad: bfloat16 [12288, 2048], P(('wide', 'narrow'))
- lang_grad: float32 [2048, 7], P(('wide', 'narrow'))
- norm1_gain_grad: float32 [2048], P(('wide', 'narrow'))
- norm1_bias_grad: float32 [2048], P(('wide', 'narrow'))
- qkv_weight_grad: float32 [6144, 2048], P(('wide', 'narrow'))
- qkv_bias_grad: float32 [6144], P(('wide', 'narrow'))
- out_weight_grad: float32 [2048, 2048], P(('wide', 'narrow'))
- norm2_gain_grad: float32 [2048], P(('wide', 'narrow'))
- norm2_bias_grad: float32 [2048], P(('wide', 'narrow'))
- gate_up_grad: float32 [11264, 2048], P(('wide', 'narrow'))
- down_grad: float32 [2048, 5632], P(('wide', 'narrow'))
The draws below stay inside these ranges and needn't reach their ends.
Inputs may be any that keep to these rules, and one draw needn't show every extreme that they name: `segment_ids`: within each packed sequence segment ids start at 0 and never fall; a document has 1 to 192 tokens, one exactly that many.
All inputs are finite; a program needn't handle non-finite values.
Results may differ from the reference program's by a relative error of at most 0.013.
Values may be sent and summed in bfloat16 or wider, within the bound.
No kernel may reach another device: no remote copies, remote signals or barrier semaphores. Data moves between devices by JAX's collectives and lax.ppermute only.
A program may use at most 448 MiB of HBM per device.

```python
import math
import jax
import jax.numpy as jnp
import numpy as np
from jax import lax

D = 2048
H = 32
HD = 64
ROT = 16
FF = 5632
LANGS = 7
TOK_DEV = 384
ROWS = 32
TOKENS = 12288
N_WIDE = 16
N_NARROW = 2


def with_ends(array, key, least, largest):
    shape = array.shape
    spot = [jax.random.randint(jax.random.fold_in(key, axis), (), 0, shape[axis]) for axis in range(len(shape))]
    array = array.at[tuple(spot)].set(least)
    longest = shape.index(max(shape))
    spot[longest] = (spot[longest] + 1) % shape[longest]
    return array.at[tuple(spot)].set(largest)


def strengthened(array, rng, source, target, blocks, factor):
    def block_of(dim):
        return (jnp.arange(array.shape[dim]) // (array.shape[dim] // blocks)).reshape((-1,) + (1,) * (array.ndim - 1 - dim))

    one_side = jax.random.permutation(rng, blocks)[block_of(target)]
    other_side = (block_of(target) + blocks // 2) % blocks
    return jnp.where((block_of(source) == one_side) | (block_of(source) == other_side), factor * array, array)


def steps_of(key, dims, cuts, least, high):
    def one(axis_at, blocks):
        draws = jax.random.uniform(jax.random.fold_in(jax.random.fold_in(key, 6), axis_at), (blocks,), jnp.float32, least / len(cuts), high / len(cuts))
        return jnp.repeat(jnp.exp(draws), dims[axis_at] // blocks).reshape((-1,) + (1,) * (len(dims) - axis_at - 1))

    factor_of = one(*cuts[0])
    for cut in cuts[1:]:
        factor_of = factor_of * one(*cut)
    return factor_of


def split_up(count, total, bound, lean):
    loads = [(1 << 20) // math.isqrt(grade ** lean) + 1 for grade in range(2, count + 1)]
    surplus, holding = total - bound - (count - 1), [1] * (count - 1)
    while surplus > 0:
        movable = [i for i in range(count - 1) if holding[i] < bound]
        mass, budget = sum([loads[i] for i in movable]), surplus
        for i in movable:
            addition = min(bound - holding[i], max(1, budget * loads[i] // mass), surplus)
            holding[i] = holding[i] + addition
            surplus = surplus - addition
    return np.array([bound] + holding)


def uneven_parts(key, amount, total, bound, lean):
    if amount == 2:
        one = jax.random.randint(key, (), max(1, total - bound), min(bound, total - 1) + 1)
        return jnp.stack([one, total - one])
    tallies = jnp.asarray(split_up(amount, total, bound, lean), jnp.int32)
    couples = (amount - 1) // 2
    source_of, sink = tallies[1:1 + 2 * couples:2], tallies[2:2 + 2 * couples:2]
    margin = jnp.minimum(source_of - 1, bound - sink)
    moved = jax.random.randint(jax.random.fold_in(key, 1), (couples,), 0, 1 << 20) % (margin + 1)
    tallies = tallies.at[1:1 + 2 * couples:2].set(source_of - moved).at[2:2 + 2 * couples:2].set(sink + moved)
    return tallies[jax.random.permutation(jax.random.fold_in(key, 2), amount)]


def gaussian(stream_key, shape, spread, reach, split=(), held_as=jnp.bfloat16):
    array = jax.random.normal(stream_key, shape, jnp.float32) * spread
    if len(split) > 0:
        array = steps_of(stream_key, shape, split, -0.22, 0.18) * array
    return jnp.clip(array, min=-reach, max=reach).astype(held_as)


def noise_with(own_key, shape, spread, bound, cuts, heavy, held_as=jnp.bfloat16):
    array = spread * jax.random.normal(own_key, shape, jnp.float32)
    if cuts:
        array = array * steps_of(own_key, shape, cuts, -0.22, 0.18)
    return jnp.clip(strengthened(array, jax.random.fold_in(own_key, 3), *heavy), -bound, bound).astype(held_as)


def setup_inputs(seed: int = 0) -> dict:
    arg_keys = jax.random.split(jax.random.key(seed), 15)
    return {
        "tokens": gaussian(arg_keys[0], (TOKENS, D), 1.0, 6.0, ((0, 32),)),
        "segment_ids": jax.vmap(lambda own: jnp.searchsorted(jnp.cumsum(uneven_parts(own, max(3, TOK_DEV // 64), TOK_DEV, TOK_DEV // 2, 2)), jnp.arange(TOK_DEV), side="right"))(jax.random.split(arg_keys[1], ROWS)).reshape((ROWS, TOK_DEV)).astype(jnp.int32),
        "language_ids": with_ends(jax.random.randint(arg_keys[2], (ROWS, TOK_DEV), 0, LANGS), jax.random.fold_in(arg_keys[2], 1), 0, LANGS - 1).astype(jnp.int32),
        "lang_table": gaussian(arg_keys[3], (D, LANGS), 0.5, 3.0, ((0, 32),)),
        "norm1_gain": jnp.clip(1.0 + 0.1 * jax.random.normal(arg_keys[4], (D,), jnp.float32), 0.5, 1.5).astype(jnp.bfloat16),
        "norm1_bias": gaussian(arg_keys[5], (D,), 0.2, 1.0, ((0, 32),)),
        "qkv_weight": gaussian(arg_keys[6], (3 * D, D), D ** -0.5, 0.125, ((0, 32),)),
        "qkv_bias": gaussian(arg_keys[7], (3 * D,), 0.3, 1.5, ((0, 32),)),
        "out_weight": gaussian(arg_keys[8], (D, D), (D // 32) ** -0.5, 0.75, ((0, 32),)),
        "norm2_gain": jnp.clip(1.0 + 0.1 * jax.random.normal(arg_keys[9], (D,), jnp.float32), 0.5, 1.5).astype(jnp.bfloat16),
        "norm2_bias": gaussian(arg_keys[10], (D,), 0.2, 1.0, ((0, 32),)),
        "gate_up_weight": gaussian(arg_keys[11], (2 * FF, D), D ** -0.5, 0.125, ((0, 32),)),
        "down_weight": gaussian(arg_keys[12], (D, FF), FF ** -0.5, 0.078125, ((0, 32),)),
        "cotangent": noise_with(arg_keys[13], (TOKENS, D), 1.0, 6.0, ((0, 32),), (0, 1, 32, 2.75)),
    }


NEG_FILL = -1e+30
NORM_EPS = 1e-05
THETA_LOG = math.log(10000.0)
HIGHEST = lax.Precision.HIGHEST

@jax.custom_vjp
def low(v):
    return lax.optimization_barrier(v.astype(jnp.bfloat16)).astype(jnp.float32)

@jax.custom_vjp
def low_back(v):
    return v

def low_keep(v):
    return (low(v), None)

def low_pass(kept, grad):
    return (grad,)

def back_keep(v):
    return (v, None)

def back_low(kept, grad):
    return (low(grad),)
low.defvjp(low_keep, low_pass)
low_back.defvjp(back_keep, back_low)

def layer_norm(values, gain_vec, bias_vec):
    centre = lax.optimization_barrier(jnp.mean(values, axis=-1, keepdims=True))
    centred = values - centre
    inv_std = lax.rsqrt(lax.optimization_barrier(jnp.mean(centred * centred, axis=-1, keepdims=True)) + NORM_EPS)
    normed = centred * inv_std
    return (normed * gain_vec.astype(jnp.float32) + bias_vec.astype(jnp.float32), normed, inv_std)

def rotary_tables(segment_row):
    count_tok = segment_row.shape[0]
    earlier = lax.optimization_barrier(jnp.sum((segment_row[None, :] < segment_row[:, None]).astype(jnp.int32), axis=1))
    places = (jnp.arange(count_tok, dtype=jnp.int32) - earlier).astype(jnp.float32)
    frequency = jnp.exp(jnp.arange(ROT // 2, dtype=jnp.float32) * (-2.0 * THETA_LOG / ROT))
    angles = places[:, None] * frequency[None, :]
    return (jnp.cos(angles), jnp.sin(angles))

def rotate(field, cosine, sine_tab, sign_val):
    half_rot = ROT // 2
    first_half = field[..., :half_rot]
    second_half = field[..., half_rot:ROT]
    cos_b = cosine[:, None, :]
    sin_b = sign_val * sine_tab[:, None, :]
    return jnp.concatenate([first_half * cos_b - second_half * sin_b, second_half * cos_b + first_half * sin_b, field[..., ROT:]], axis=-1)

def layer(x_in, table, gain1, bias1, w_qkv, b_qkv, w_out, gain2, bias2, w_gu, w_down, lang_row, allowed, cosine, sine_tab):
    count_tok = x_in.shape[0]
    stream0 = x_in + table[:, lang_row].T
    normed_in = low(layer_norm(stream0, gain1, bias1)[0])
    projected = low_back(jnp.dot(normed_in, w_qkv.T, precision=HIGHEST) + b_qkv)
    query = low(rotate(projected[:, :D].reshape(count_tok, H, HD), cosine, sine_tab, 1.0))
    key_rot = low(rotate(projected[:, D:2 * D].reshape(count_tok, H, HD), cosine, sine_tab, 1.0))
    value_in = low(projected[:, 2 * D:].reshape(count_tok, H, HD))
    scores = low_back(jnp.einsum('qhd,khd->hqk', query, key_rot, precision=HIGHEST) * (1.0 / math.sqrt(HD)))
    scores = jnp.where(allowed[None], scores, NEG_FILL)
    row_max = lax.optimization_barrier(jnp.max(scores, axis=-1, keepdims=True))
    unnormed = jnp.exp(scores - row_max)
    attn_probs = low(unnormed / lax.optimization_barrier(jnp.sum(unnormed, axis=-1, keepdims=True)))
    attended = jnp.einsum('hqk,khd->qhd', attn_probs, value_in, precision=HIGHEST).reshape(count_tok, D)
    attended = low(low_back(attended))
    stream1 = stream0 + low_back(jnp.dot(attended, w_out.T, precision=HIGHEST))
    normed_mid = low(layer_norm(stream1, gain2, bias2)[0])
    gate_up = low_back(jnp.dot(normed_mid, w_gu.T, precision=HIGHEST))
    gate_part = gate_up[:, :FF]
    hidden = low(gate_part * jax.nn.sigmoid(gate_part) * gate_up[:, FF:])
    return stream1 + low_back(jnp.dot(hidden, w_down.T, precision=HIGHEST))

def reference(tokens, segment_ids, language_ids, lang_table, norm1_gain, norm1_bias, qkv_weight, qkv_bias, out_weight, norm2_gain, norm2_bias, gate_up_weight, down_weight, cotangent):
    row_count = N_WIDE * N_NARROW
    params = tuple((weight_arr.astype(jnp.float32) for weight_arr in (lang_table, norm1_gain, norm1_bias, qkv_weight, qkv_bias, out_weight, norm2_gain, norm2_bias, gate_up_weight, down_weight)))
    tok_rows = tokens.astype(jnp.float32).reshape(row_count, TOK_DEV, D)
    cot_rows = cotangent.astype(jnp.float32).reshape(row_count, TOK_DEV, D)

    def step(totals, row_items):
        tok_row, seg_row, lang_row, cot_row = row_items
        cosine, sine_tab = rotary_tables(seg_row)
        positions = jnp.arange(TOK_DEV, dtype=jnp.int32)
        allowed = (seg_row[:, None] == seg_row[None, :]) & (positions[None, :] <= positions[:, None])

        def apply_layer(x_in, *weights):
            return layer(x_in, *weights, lang_row, allowed, cosine, sine_tab)
        mixed_row, pull_back = jax.vjp(apply_layer, tok_row, *params)
        grads = pull_back(cot_row)
        new_totals = tuple((running + fresh for running, fresh in zip(totals, grads[1:])))
        return (new_totals, (mixed_row.astype(jnp.bfloat16), grads[0].astype(jnp.bfloat16)))
    init = tuple((jnp.zeros_like(weight_arr) for weight_arr in params))
    totals, outputs = lax.scan(step, init, (tok_rows, segment_ids, language_ids, cot_rows))
    mixed = outputs[0].reshape(TOKENS, D)
    token_grad = outputs[1].reshape(TOKENS, D)
    return (mixed, token_grad, totals[0], totals[1], totals[2], totals[3], totals[4], totals[5], totals[6], totals[7], totals[8], totals[9])
```

```python
import functools
import math

import jax
import jax.numpy as jnp
from jax import lax
from jax.experimental import pallas as pl
from jax.experimental.pallas import tpu as pltpu
from jax.sharding import PartitionSpec as P

D = 2048
H = 32
HD = 64
ROT = 16
FF = 5632
LANGS = 7

NEG_FILL = -1e30
NORM_EPS = 1e-05
THETA_LOG = math.log(10000.0)
AXES = ("wide", "narrow")
BF = jnp.bfloat16
F32 = jnp.float32
HEADS_STEP = 4
LANES = HEADS_STEP * HD
Q_BLOCK = 128
SMALL_ROWS = LANGS + 4 + 3
SHORT = pl.CostEstimate(flops=1, bytes_accessed=1, transcendentals=0)


def layer_norm(values, gain_vec, bias_vec):
    centre = jnp.mean(values, axis=-1, keepdims=True)
    centred = values - centre
    inv_std = lax.rsqrt(jnp.mean(centred * centred, axis=-1, keepdims=True) + NORM_EPS)
    normed = centred * inv_std
    return (normed * gain_vec.astype(F32) + bias_vec.astype(F32), normed, inv_std)


def norm_back(grad_out, normed, inv_std, gain_vec):
    scaled = grad_out * gain_vec.astype(F32)
    inner = (
        scaled
        - jnp.mean(scaled, axis=-1, keepdims=True)
        - normed * jnp.mean(scaled * normed, axis=-1, keepdims=True)
    )
    return (inv_std * inner, jnp.sum(grad_out * normed, axis=0), jnp.sum(grad_out, axis=0))


def rotary_tables(segment_row):
    count_tok = segment_row.shape[0]
    earlier = jnp.sum((segment_row[None, :] < segment_row[:, None]).astype(jnp.int32), axis=1)
    places = (jnp.arange(count_tok, dtype=jnp.int32) - earlier).astype(F32)
    frequency = jnp.exp(jnp.arange(ROT // 2, dtype=F32) * (-2.0 * THETA_LOG / ROT))
    angles = places[:, None] * frequency[None, :]
    cosine, sine = jnp.cos(angles), jnp.sin(angles)
    rest = HD - ROT
    half = jnp.zeros((count_tok, ROT // 2), F32)
    none = jnp.zeros((count_tok, rest), F32)
    cos_head = jnp.concatenate([cosine, cosine, none + 1.0], axis=1)
    first_head = jnp.concatenate([-sine, half, none], axis=1)
    second_head = jnp.concatenate([half, sine, none], axis=1)
    return tuple(jnp.tile(t, (1, HEADS_STEP)) for t in (cos_head, first_head, second_head))


def mul_rows(left, weight):
    return lax.dot_general(left, weight, (((1,), (1,)), ((), ())), preferred_element_type=F32)


def weight_grad(grad_rows, inputs):
    return lax.dot_general(grad_rows, inputs, (((0,), (0,)), ((), ())), preferred_element_type=F32)


def shifts(field):
    half = ROT // 2
    return (pltpu.roll(field, LANES - half, 1), pltpu.roll(field, half, 1))


def lane_masks(scale):
    head_of = lax.broadcasted_iota(jnp.int32, (1, LANES), 1) // HD
    return [jnp.where(head_of == head, scale, 0.0).astype(BF) for head in range(HEADS_STEP)]


def by_head(rows, masks):
    return jnp.concatenate([rows * mask for mask in masks], axis=0)


def joined(field, masks):
    parts = jnp.split(field, HEADS_STEP, axis=0)
    return sum(part * mask.astype(F32) for part, mask in zip(parts, masks))


def probs_of(queries, keys, allowed):
    scores = jnp.where(allowed, mul_rows(keys, queries), NEG_FILL)
    unnormed = jnp.exp(scores - jnp.max(scores, axis=0, keepdims=True))
    return unnormed * (1.0 / jnp.sum(unnormed, axis=0, keepdims=True))


def allowed_of(seg_col, seg_row, block):
    start, end = block * Q_BLOCK, (block + 1) * Q_BLOCK
    key_at = lax.broadcasted_iota(jnp.int32, (end, Q_BLOCK), 0)
    query_at = lax.broadcasted_iota(jnp.int32, (end, Q_BLOCK), 1) + start
    one = (seg_col[:end, :] == seg_row[:, start:end]) & (key_at <= query_at)
    return jnp.concatenate([one] * HEADS_STEP, axis=1)


def attend_kernel(
    x_ref, wq_ref, wk_ref, wv_ref, bq_ref, bk_ref, bv_ref, cos_ref, first_ref, second_ref,
    segc_ref, segr_ref, q_ref, k_ref, v_ref, out_ref,
):
    x_in = x_ref[...]
    cosine, first, second = cos_ref[...], first_ref[...], second_ref[...]

    def turned(w_ref, b_ref):
        field = mul_rows(x_in, w_ref[...]) + b_ref[...]
        ahead, behind = shifts(field)
        return (field * cosine + ahead * first + behind * second).astype(BF)

    q_ref[...] = turned(wq_ref, bq_ref)
    k_ref[...] = turned(wk_ref, bk_ref)
    v_ref[...] = (mul_rows(x_in, wv_ref[...]) + bv_ref[...]).astype(BF)
    scaled, masks = lane_masks(1.0 / math.sqrt(HD)), lane_masks(1.0)
    seg_col, seg_row = segc_ref[...], segr_ref[...]
    for block in range(x_in.shape[0] // Q_BLOCK):
        start, end = block * Q_BLOCK, (block + 1) * Q_BLOCK
        queries = by_head(q_ref[start:end, :], scaled)
        probs = probs_of(queries, k_ref[:end, :], allowed_of(seg_col, seg_row, block))
        out_ref[start:end, :] = joined(weight_grad(probs.astype(BF), v_ref[:end, :]), masks).astype(BF)


def attend_back_kernel(
    q_ref, k_ref, v_ref, g_ref, cos_ref, first_ref, second_ref, segc_ref, segr_ref, *rest
):
    grad_ref, dk_sum, dv_sum = rest[-3:]
    cosine, first, second = cos_ref[...], first_ref[...], second_ref[...]
    scale = 1.0 / math.sqrt(HD)
    width = grad_ref.shape[1] // 3

    def columns(which):
        return pl.ds(pl.multiple_of(which * width + pl.program_id(1) * LANES, LANES), LANES)

    def turned_back(field, start, end):
        ahead, behind = shifts(field)
        turned = field * cosine[start:end] - ahead * first[start:end] - behind * second[start:end]
        return turned.astype(BF)

    dk_sum[...] = jnp.zeros_like(dk_sum)
    dv_sum[...] = jnp.zeros_like(dv_sum)
    scaled, masks = lane_masks(scale), lane_masks(1.0)
    seg_col, seg_row = segc_ref[...], segr_ref[...]
    for block in range(q_ref.shape[0] // Q_BLOCK):
        start, end = block * Q_BLOCK, (block + 1) * Q_BLOCK
        keys, values = k_ref[:end, :], v_ref[:end, :]
        queries = by_head(q_ref[start:end, :], scaled)
        grads = by_head(g_ref[start:end, :], masks)
        probs = probs_of(queries, keys, allowed_of(seg_col, seg_row, block))
        grad_probs = mul_rows(values, grads)
        dots = jnp.sum(probs * grad_probs, axis=0, keepdims=True)
        grad_scores = (probs * (grad_probs - dots)).astype(BF)
        dv_sum[:end, :] += jnp.dot(probs.astype(BF), grads, preferred_element_type=F32)
        dk_sum[:end, :] += jnp.dot(grad_scores, queries, preferred_element_type=F32)
        dq_rows = joined(weight_grad(grad_scores, keys), masks) * scale
        grad_ref[start:end, columns(0)] = turned_back(dq_rows, start, end)
    grad_ref[:, columns(1)] = turned_back(dk_sum[...], 0, dk_sum.shape[0])
    grad_ref[:, columns(2)] = dv_sum[...].astype(BF)


def of_sequence(shape):
    return pl.BlockSpec(shape, lambda step, seq: (seq, 0))


def row_of_sequence(count_tok):
    return pl.BlockSpec((None, 1, count_tok), lambda step, seq: (seq, 0, 0))


def attend(normed_in, weight, bias_row, tables, seg_col, seg_row):
    count_tok = seg_row.shape[2]
    rows, cols = normed_in.shape[0], weight.shape[0] // 3
    steps = cols // LANES
    head_cols = pl.BlockSpec((count_tok, LANES), lambda step, seq: (seq, step))

    def part(which):
        return pl.BlockSpec((LANES, D), lambda step, seq: (which * steps + step, 0))

    def bias_part(which):
        return pl.BlockSpec((1, LANES), lambda step, seq: (0, which * steps + step))

    return pl.pallas_call(
        attend_kernel,
        grid=(steps, rows // count_tok),
        in_specs=[of_sequence((count_tok, D))]
        + [part(i) for i in range(3)]
        + [bias_part(i) for i in range(3)]
        + [of_sequence((count_tok, LANES))] * 3
        + [of_sequence((count_tok, 1)), row_of_sequence(count_tok)],
        out_specs=[head_cols] * 4,
        out_shape=[jax.ShapeDtypeStruct((rows, cols), BF)] * 4,
        compiler_params=pltpu.CompilerParams(vmem_limit_bytes=48 << 20),
        cost_estimate=SHORT,
        name="attend",
    )(normed_in, weight, weight, weight, bias_row, bias_row, bias_row, *tables, seg_col, seg_row)


def attend_back(query, key_rot, value_in, grad_attended, tables, seg_col, seg_row, first_seq, others):
    count_tok = seg_row.shape[2]
    rows, cols = grad_attended.shape

    def of_heads(first):
        return pl.BlockSpec((count_tok, LANES), lambda seq, step: (seq + first, step))

    def of_seq(shape):
        return pl.BlockSpec(shape, lambda seq, step: (seq + first_seq, 0))

    operands = [query, key_rot, value_in, grad_attended, *tables, seg_col, seg_row]
    in_specs = (
        [of_heads(first_seq)] * 3
        + [of_heads(0)]
        + [of_seq((count_tok, LANES))] * 3
        + [of_seq((count_tok, 1))]
        + [pl.BlockSpec((None, 1, count_tok), lambda seq, step: (seq + first_seq, 0, 0))]
    )
    aliases = {}
    if others is not None:
        aliases = {len(operands): 0}
        operands.append(others)
        in_specs.append(pl.BlockSpec(memory_space=pl.ANY))
    return pl.pallas_call(
        attend_back_kernel,
        grid=(rows // count_tok, cols // LANES),
        in_specs=in_specs,
        out_specs=of_seq((count_tok, 3 * cols)),
        out_shape=jax.ShapeDtypeStruct((query.shape[0], 3 * cols), BF),
        scratch_shapes=[pltpu.VMEM((count_tok, LANES), F32)] * 2,
        input_output_aliases=aliases,
        compiler_params=pltpu.CompilerParams(vmem_limit_bytes=48 << 20),
        cost_estimate=SHORT,
        name="attend_back",
    )(*operands)


def rows_product(left, right, first_row, count_rows, right_rows=False):
    inner, cols = right.shape[::-1] if right_rows else right.shape
    width = 512

    def kernel(left_ref, right_ref, out_ref):
        if right_rows:
            out_ref[...] = mul_rows(left_ref[...], right_ref[...])
        else:
            out_ref[...] = jnp.dot(left_ref[...], right_ref[...], preferred_element_type=F32)

    if right_rows:
        right_spec = pl.BlockSpec((width, inner), lambda n: (n, 0))
    else:
        right_spec = pl.BlockSpec((inner, width), lambda n: (0, n))
    return pl.pallas_call(
        kernel,
        grid=(cols // width,),
        in_specs=[
            pl.BlockSpec((count_rows, inner), lambda n: (first_row // count_rows, 0)),
            right_spec,
        ],
        out_specs=pl.BlockSpec((count_rows, width), lambda n: (0, n)),
        out_shape=jax.ShapeDtypeStruct((count_rows, cols), F32),
        compiler_params=pltpu.CompilerParams(vmem_limit_bytes=48 << 20),
        cost_estimate=SHORT,
        name="rows_product",
    )(left, right)


def attention_grads(half, side_at, grad_proj, inputs, grad_attn, attended, line, group):
    count_rows, proj_cols = grad_proj.shape
    cols = attended.shape[1]
    qkv_rows, out_rows = proj_cols // (2 * line), D // (2 * line)
    share = out_rows // group
    width = D // 2
    members = width // cols
    rows = qkv_rows + share
    pair_rows = grad_attn[0].shape[0]

    def kernel(side_ref, proj_ref, input_ref, attended_ref, *refs):
        attn_refs, (away_ref, mine_ref) = refs[:-2], refs[-2:]
        qkv = weight_grad(proj_ref[...], input_ref[...])
        blocks = []
        for side in range(2):
            start = side * out_rows + half * (members * share)
            out = sum(
                weight_grad(
                    attn_ref[:, start : start + members * share],
                    attended_ref[pair * pair_rows : (pair + 1) * pair_rows, :],
                )
                for pair, attn_ref in enumerate(attn_refs)
            )
            out = jnp.concatenate([out[m * share : (m + 1) * share] for m in range(members)], axis=1)
            blocks.append((qkv[side * qkv_rows : (side + 1) * qkv_rows], out))

        def store(mine, away):
            mine_ref[:qkv_rows, :] = blocks[mine][0]
            mine_ref[qkv_rows:, :] = blocks[mine][1]
            away_ref[:qkv_rows, :] = blocks[away][0].astype(BF)
            away_ref[qkv_rows:, :] = blocks[away][1].astype(BF)

        pl.when(side_ref[0] == 0)(lambda: store(0, 1))
        pl.when(side_ref[0] != 0)(lambda: store(1, 0))

    out_block = pl.BlockSpec((None, rows, width), lambda z, side: (z, 0, 0))
    return pl.pallas_call(
        kernel,
        grid_spec=pltpu.PrefetchScalarGridSpec(
            num_scalar_prefetch=1,
            grid=(line,),
            in_specs=[
                pl.BlockSpec((count_rows, 2 * qkv_rows), lambda z, side: (0, z)),
                pl.BlockSpec((count_rows, width), lambda z, side: (0, half)),
                pl.BlockSpec((count_rows, cols), lambda z, side: (0, 0)),
            ]
            + [pl.BlockSpec((pair_rows, 2 * out_rows), lambda z, side: (0, z))] * len(grad_attn),
            out_specs=[out_block, out_block],
        ),
        out_shape=[
            jax.ShapeDtypeStruct((line, rows, width), BF),
            jax.ShapeDtypeStruct((line, rows, width), F32),
        ],
        compiler_params=pltpu.CompilerParams(vmem_limit_bytes=56 << 20),
        cost_estimate=SHORT,
        name="attention_grads",
    )(side_at.reshape(1), grad_proj, inputs, attended, *grad_attn)


class Layout:
    def __init__(self, n_wide, n_narrow):
        self.narrow = n_narrow
        self.count = n_wide * n_narrow
        self.group = 2 * n_narrow
        self.outer = n_wide // 2
        self.line = self.outer // 2
        self.core_mask = n_narrow
        self.side_mask = 2 * n_narrow
        self.line_mask = 4 * n_narrow
        self.shifts = list(range(1, n_narrow))
        self.outer_groups = [
            [o * self.group + member for o in range(self.outer)] for member in range(self.group)
        ]

    def swap(self, value, mask):
        return lax.ppermute(value, AXES, [(i, i ^ mask) for i in range(self.count)])


    def gather_pairs(self, value, meanwhile=None):
        own = (value, self.swap(value, self.core_mask))
        shifted = [self.swap(value, mask) for mask in self.shifts]
        done = None
        if meanwhile is not None:
            shifted, done = lax.optimization_barrier((shifted, meanwhile(own)))
        return [own] + [(block, self.swap(block, self.core_mask)) for block in shifted], done

    def across_cores(self, partials):
        summed = []
        for partial in partials:
            own, sent = jnp.split(partial, 2)
            summed.append(own + self.swap(sent.astype(BF), self.core_mask).astype(F32))
        return summed

    def across_shifts(self, summed, meanwhile=None):
        shifted = [self.swap(part.astype(BF), mask) for part, mask in zip(summed[1:], self.shifts)]
        if meanwhile is not None:
            shifted, meanwhile = lax.optimization_barrier((shifted, meanwhile))
        return sum((part.astype(F32) for part in shifted), start=summed[0]), meanwhile

    def swap_group(self, pieces, member):
        result = jnp.zeros(pieces.shape, pieces.dtype)
        for mask in range(self.group):
            piece = lax.dynamic_index_in_dim(pieces, member ^ mask, 0, keepdims=False)
            if mask:
                piece = self.swap(piece, mask)
            result = lax.dynamic_update_index_in_dim(result, piece, member ^ mask, 0)
        return result


    def gather_outer(self, value):
        return lax.all_gather(value, AXES, axis=0, axis_index_groups=self.outer_groups)

    def scatter_outer(self, value):
        return lax.psum_scatter(
            value, AXES, scatter_dimension=0, tiled=True, axis_index_groups=self.outer_groups
        )

    def by_side(self, grad, place):
        by_place = grad.reshape(self.line, 2, -1, grad.shape[1])
        away = lax.dynamic_index_in_dim(by_place, 1 - place % 2, 1, keepdims=False).astype(BF)
        return away, lax.dynamic_index_in_dim(by_place, place % 2, 1, keepdims=False)

    def across_sides(self, away, mine):
        return mine + self.swap(away, self.side_mask).astype(F32)

    def line_steps(self):
        return [1 << bit for bit in range(self.line.bit_length() - 1)]

    def along_line(self, mine, place, step):
        pairs = mine.reshape(-1, 2, *mine.shape[1:])
        at = place // 2 // step % 2
        away = lax.dynamic_index_in_dim(pairs, 1 - at, 1, keepdims=False).astype(BF)
        mine = lax.dynamic_index_in_dim(pairs, at, 1, keepdims=False)
        return mine + self.swap(away, step * self.line_mask).astype(F32)


    def gather_small(self, row, index):
        blocks = row
        mask = 1
        while mask < self.line_mask:
            blocks = jnp.concatenate([blocks, self.swap(blocks, mask)])
            mask *= 2
        blocks = jnp.concatenate(
            [blocks] + [self.swap(blocks, step * self.line_mask) for step in range(1, self.line)]
        )
        return jnp.dot(self.by_mask(index).astype(row.dtype), blocks, preferred_element_type=F32)

    def scatter_small_line(self, rows, index):
        rows = jnp.dot(self.by_mask(index).astype(F32), rows, precision=lax.Precision.HIGHEST)
        blocks = jnp.split(rows, self.line)
        total = blocks[0]
        for step in range(1, self.line):
            total = total + self.swap(blocks[step], step * self.line_mask)
        return total

    def scatter_small_rest(self, total):
        mask = self.side_mask
        while mask:
            total = total[:mask] + self.swap(total[mask:], mask)
            mask //= 2
        return total

    def by_mask(self, index):
        numbers = jnp.arange(self.count, dtype=jnp.int32)
        return (numbers[:, None] ^ numbers[None, :]) == index


def deal_heads(layout, weight, member):
    per, group = weight.shape[0] // HD, layout.group
    got = [
        lax.ppermute(
            block,
            AXES,
            [(i, i // group * group + (per * i + j) % group) for i in range(layout.count)],
        )
        for j, block in enumerate(jnp.split(weight, per))
    ]
    stacked = jnp.stack(got)
    order = [lax.rem(k * group + member, per) for k in range(per)]
    return jnp.concatenate(
        [lax.dynamic_index_in_dim(stacked, j, 0, keepdims=False) for j in order]
    )


def deal_back(layout, rows, member):
    per, group = rows.shape[0] // HD, layout.group
    blocks = rows.reshape(per, HD, rows.shape[1])
    result = []
    for j in range(per):
        chosen = blocks[0]
        for k in range(1, per):
            chosen = jnp.where(lax.rem(k * group + member, per) == j, blocks[k], chosen)
        pairs = [(i // group * group + (per * i + j) % group, i) for i in range(layout.count)]
        result.append(lax.ppermute(chosen, AXES, pairs))
    return jnp.concatenate(result)


def heads_dealt(layout, qkv_rows):
    return qkv_rows % HD == 0 and math.gcd(qkv_rows // HD, layout.group) == 1


def gather_attention(layout, qkv_weight, out_weight, member):
    qkv_rows, share = qkv_weight.shape[0], out_weight.shape[0]
    cols = D // layout.group
    out_pieces = jnp.transpose(
        out_weight.reshape(share, H // layout.group, layout.group, HD), (2, 0, 1, 3)
    ).reshape(layout.group, share, cols)
    out_mine = layout.swap_group(out_pieces, member)
    out_mine = out_mine.reshape(layout.group * share, cols)
    if not heads_dealt(layout, qkv_rows):
        full = lax.all_gather(qkv_weight, AXES, axis=0, tiled=True)
        split = full.reshape(3 * H // layout.group, layout.group, HD, D)
        mine = lax.dynamic_index_in_dim(split, member, 1, keepdims=False).reshape(-1, D)
        return mine, layout.gather_outer(out_mine).reshape(D, cols)
    both = jnp.concatenate([deal_heads(layout, qkv_weight, member), out_mine.reshape(share, D)])
    full = layout.gather_outer(both)
    return full[:, :qkv_rows].reshape(-1, D), full[:, qkv_rows:].reshape(D, cols)


def scatter_attention(layout, grad_proj, inputs, grad_attn, attended, qkv_rows, place, first, second):
    steps = layout.line_steps()
    if not heads_dealt(layout, qkv_rows):
        group = layout.group
        split = jnp.zeros((3 * H // group, group, HD, D), BF)
        grad = weight_grad(grad_proj, inputs).astype(BF).reshape(-1, 1, HD, D)
        split = lax.dynamic_update_index_in_dim(split, grad, lax.axis_index(AXES) % group, 1)
        qkv_sum = lax.psum_scatter(split.reshape(-1, D), AXES, scatter_dimension=0, tiled=True)
        out_own = weight_grad(jnp.concatenate(grad_attn), attended)
        out_sum = layout.across_sides(*layout.by_side(out_own, place))
        for step in steps:
            out_sum = layout.along_line(out_sum, place, step)
        return qkv_sum, out_sum[0].astype(BF), second(first(grad_proj))
    others = (inputs, grad_attn, attended, layout.line, layout.group)
    away, mine = attention_grads(0, place % 2, grad_proj, *others)
    away, mine, grad_proj = lax.optimization_barrier((away, mine, grad_proj))
    left = layout.across_sides(away, mine)
    away, mine = attention_grads(1, place % 2, grad_proj, *others)
    left, away, mine, done = lax.optimization_barrier((left, away, mine, first(grad_proj)))
    left = layout.along_line(left, place, steps[0])
    right = layout.across_sides(away, mine)
    left, right, done = lax.optimization_barrier((left, right, second(done)))
    for step in steps[1:]:
        left = layout.along_line(left, place, step)
    right = layout.along_line(right, place, steps[0])
    left, right, last = lax.optimization_barrier((left, right, done[0]))
    done = (last, *done[1:])
    for step in steps[1:]:
        right = layout.along_line(right, place, step)
    summed = jnp.concatenate([left[0].astype(BF), right[0].astype(BF)], axis=1)
    out_sum = summed[qkv_rows:].reshape(-1, layout.group, D // layout.group)
    return summed[:qkv_rows], jnp.transpose(out_sum, (1, 0, 2)).reshape(-1, D // layout.group), done


def per_device(
    layout,
    tokens,
    segment_ids,
    language_ids,
    lang_table,
    norm1_gain,
    norm1_bias,
    qkv_weight,
    qkv_bias,
    out_weight,
    norm2_gain,
    norm2_bias,
    gate_up_weight,
    down_weight,
    cotangent,
):
    count_tok = tokens.shape[0]
    group, outer, count, narrow = layout.group, layout.outer, layout.count, layout.narrow
    index = lax.axis_index(AXES)
    member, place = lax.rem(index, group), index // group
    share = D // count
    unit_rows = gate_up_weight.shape[0]
    units = FF // group
    head_cols = D // group

    small = jnp.concatenate(
        [
            lang_table.T,
            norm1_gain[None],
            norm1_bias[None],
            norm2_gain[None],
            norm2_bias[None],
            qkv_bias.reshape(3, share),
        ]
    )
    small_len = SMALL_ROWS * share
    small_all = layout.gather_small(small.reshape(1, small_len), index)
    small_all = small_all.reshape(count, SMALL_ROWS, share)
    small_rows = jnp.transpose(small_all, (1, 0, 2)).reshape(SMALL_ROWS, D)
    table_rows = small_rows[:LANGS].astype(BF)
    gain1, bias1, gain2, bias2 = (small_rows[LANGS + i] for i in range(4))
    bias_heads = small_all[:, LANGS + 4 :].reshape(3, H // group, group, HD)
    bias_row = lax.dynamic_index_in_dim(bias_heads, member, 2, keepdims=False).reshape(
        1, 3 * head_cols
    )

    qkv_part, out_part = gather_attention(layout, qkv_weight, out_weight, member)
    gate_up_part = layout.gather_outer(gate_up_weight).reshape(2 * units, D)
    down_pieces = jnp.transpose(
        down_weight.reshape(share, outer // 2, group, unit_rows), (2, 0, 1, 3)
    ).reshape(group, share, units)
    down_mine = layout.swap_group(down_pieces, member).reshape(group * share, units)

    segment_pairs, _ = layout.gather_pairs(segment_ids)
    segment_rows = [row for pair in segment_pairs for row in pair]
    seg_row = jnp.stack(segment_rows)
    seg_col = seg_row.reshape(group * count_tok, 1)
    tables = tuple(
        jnp.concatenate(parts) for parts in zip(*(rotary_tables(row[0]) for row in segment_rows))
    )
    one_hot = language_ids[0][:, None] == jnp.arange(LANGS, dtype=jnp.int32)[None, :]
    stream0 = tokens.astype(F32) + jnp.dot(
        one_hot.astype(BF), table_rows, preferred_element_type=F32
    )
    normed_in, norm1_hat, norm1_inv = layer_norm(stream0, gain1, bias1)
    in_pairs, _ = layout.gather_pairs(normed_in.astype(BF))
    in_group = jnp.concatenate(sum(in_pairs, ()))
    in_group, cotangent_late, down_mine = lax.optimization_barrier((in_group, cotangent, down_mine))
    down_part = layout.gather_outer(down_mine).reshape(D, units)
    cot_pairs, _ = layout.gather_pairs(cotangent_late)
    cot_group = jnp.concatenate(sum(cot_pairs, ()))
    query, key_rot, value_in, attended = attend(
        in_group, qkv_part, bias_row, tables, seg_col, seg_row
    )
    attended, cot_group = lax.optimization_barrier((attended, cot_group))
    pair_rows = 2 * count_tok

    def pair_of(value, pair):
        return value[pair * pair_rows : (pair + 1) * pair_rows]

    out_sums = layout.across_cores(
        [mul_rows(pair_of(attended, pair), out_part) for pair in range(narrow)]
    )
    stream1 = stream0 + layout.across_shifts(out_sums)[0]

    normed_mid, norm2_hat, norm2_inv = layer_norm(stream1, gain2, bias2)
    mid_pairs, _ = layout.gather_pairs(normed_mid.astype(BF))
    mid_group = jnp.concatenate(sum(mid_pairs, ()))
    gate_up = mul_rows(mid_group, gate_up_part)
    gate_part, up_part = gate_up[:, :units], gate_up[:, units:]
    sigma_gate = jax.nn.sigmoid(gate_part)
    silu_gate = gate_part * sigma_gate
    hidden = (silu_gate * up_part).astype(BF)
    down_own = weight_grad(cot_group, hidden).astype(BF)
    down_part, down_own = lax.optimization_barrier((down_part, down_own))
    down_sum = layout.scatter_outer(down_own)
    grad_hidden = jnp.dot(cot_group, down_part, preferred_element_type=F32)
    grad_gate = grad_hidden * up_part * (sigma_gate + gate_part * sigma_gate * (1.0 - sigma_gate))
    grad_gu = jnp.concatenate([grad_gate, grad_hidden * silu_gate], axis=1).astype(BF)
    mid_parts = {}
    for pair in reversed(range(narrow)):
        grad_rows = pair_of(grad_gu, pair)
        if pair + 1 in mid_parts:
            grad_rows, mid_parts[pair + 1] = lax.optimization_barrier((grad_rows, mid_parts[pair + 1]))
        mid_parts[pair] = jnp.dot(grad_rows, gate_up_part, preferred_element_type=F32)
    mid_sums = layout.across_cores([mid_parts[pair] for pair in range(narrow)])
    gate_up_own = weight_grad(grad_gu, mid_group).astype(BF)
    grad_mid, gate_up_own = layout.across_shifts(mid_sums, gate_up_own)
    gate_up_sum = layout.scatter_outer(gate_up_own)

    grad_norm2, gain2_grad, bias2_grad = norm_back(grad_mid, norm2_hat, norm2_inv, gain2)
    grad_stream1 = cotangent.astype(F32) + grad_norm2

    def back_of(pair, first_seq, others):
        grad_rows = jnp.concatenate(pair)
        grad_attended = jnp.dot(grad_rows, out_part, preferred_element_type=F32).astype(BF)
        grads = attend_back(
            query, key_rot, value_in, grad_attended, tables, seg_col, seg_row, first_seq, others
        )
        return grads, grad_rows

    def in_the_meantime(pair):
        return back_of(pair, 0, None)

    attn_pairs, (grad_proj, own_rows) = layout.gather_pairs(
        grad_stream1.astype(BF), in_the_meantime
    )
    grad_attn = [own_rows]
    for pair in range(1, narrow):
        grad_proj, grad_rows = back_of(attn_pairs[pair], 2 * pair, grad_proj)
        grad_attn.append(grad_rows)

    def input_grad(grad_proj):
        parts = [
            rows_product(grad_proj, qkv_part, pair * pair_rows, pair_rows) for pair in range(narrow)
        ]
        return layout.across_shifts(layout.across_cores(parts))[0], hidden

    def first_norm(grad_in):
        grad_norm1, gain1_grad, bias1_grad = norm_back(grad_in, norm1_hat, norm1_inv, gain1)
        grad_stream0 = grad_stream1 + grad_norm1
        lang_grad = lax.dot_general(
            one_hot.astype(F32),
            grad_stream0,
            (((0,), (0,)), ((), ())),
            precision=lax.Precision.HIGHEST,
        )
        bias_grad = jnp.zeros((3 * H // group, group, HD), F32)
        bias_grad = lax.dynamic_update_index_in_dim(
            bias_grad, jnp.sum(grad_proj.astype(F32), axis=0).reshape(-1, 1, HD), member, 1
        )
        rows = jnp.concatenate(
            [lang_grad, jnp.stack([gain1_grad, bias1_grad, gain2_grad, bias2_grad])]
        ).reshape(LANGS + 4, count, share)
        small_grad = jnp.concatenate(
            [jnp.transpose(rows, (1, 0, 2)), bias_grad.reshape(count, 3, share)], axis=1
        ).reshape(count, small_len)
        return grad_stream0.astype(BF), small_grad

    def meanwhile(done):
        grad_in, hidden = done
        token_grad, small_grad = first_norm(grad_in)
        small_line = layout.scatter_small_line(small_grad, index)
        mixed_parts = [
            rows_product(hidden, down_part, pair * pair_rows, pair_rows, right_rows=True)
            for pair in range(narrow)
        ]
        down_got = layout.swap_group(down_sum.reshape(group, share, units), member)
        return small_line, token_grad, mixed_parts, gate_up_sum, down_got

    qkv_sum, out_sum, (small_line, token_grad, mixed_parts, gate_up_sum, down_got) = scatter_attention(
        layout, grad_proj, in_group, grad_attn, attended, qkv_weight.shape[0], place, input_grad, meanwhile
    )
    mixed_sums = layout.across_cores(mixed_parts)
    small_sum = layout.scatter_small_rest(small_line).reshape(SMALL_ROWS, share)
    mixed = (stream1 + layout.across_shifts(mixed_sums)[0]).astype(BF)

    if heads_dealt(layout, qkv_weight.shape[0]):
        qkv_sum = deal_back(layout, qkv_sum, member)
    down_grad = jnp.transpose(
        down_got.reshape(group, share, outer // 2, unit_rows), (1, 2, 0, 3)
    ).reshape(share, FF)
    out_got = layout.swap_group(out_sum.reshape(group, share, head_cols), member)
    out_grad = jnp.transpose(
        out_got.reshape(group, share, H // group, HD), (1, 2, 0, 3)
    ).reshape(share, D)
    return (
        mixed,
        token_grad,
        small_sum[:LANGS].T,
        small_sum[LANGS],
        small_sum[LANGS + 1],
        qkv_sum.astype(F32),
        small_sum[LANGS + 4 :].reshape(3 * share),
        out_grad.astype(F32),
        small_sum[LANGS + 2],
        small_sum[LANGS + 3],
        gate_up_sum.astype(F32),
        down_grad.astype(F32),
    )


def solution(mesh):
    rows, vector = P(AXES, None), P(AXES)
    layout = Layout(mesh.shape["wide"], mesh.shape["narrow"])
    return jax.shard_map(
        functools.partial(per_device, layout),
        mesh=mesh,
        in_specs=(rows, rows, rows, rows, vector, vector, rows, vector, rows, vector, vector, rows, rows, rows),
        out_specs=(rows, rows, rows, vector, vector, rows, vector, rows, vector, vector, rows, rows),
        check_vma=False,
    )
```

```python
import functools
import math

import jax
import jax.numpy as jnp
from jax import lax
from jax.experimental import pallas as pl
from jax.experimental.pallas import tpu as pltpu
from jax.sharding import PartitionSpec as P

D = 2048
H = 32
HD = 64
ROT = 16
FF = 5632
LANGS = 7

NEG_FILL = -1e30
NORM_EPS = 1e-05
THETA_LOG = math.log(10000.0)
AXES = ("wide", "narrow")
BF = jnp.bfloat16
F32 = jnp.float32
HEADS_STEP = 4
LANES = HEADS_STEP * HD
Q_BLOCK = 128
SMALL_ROWS = LANGS + 4 + 3
SHORT = pl.CostEstimate(flops=1, bytes_accessed=1, transcendentals=0)


def layer_norm(values, gain_vec, bias_vec):
    centre = jnp.mean(values, axis=-1, keepdims=True)
    centred = values - centre
    inv_std = lax.rsqrt(jnp.mean(centred * centred, axis=-1, keepdims=True) + NORM_EPS)
    normed = centred * inv_std
    return (normed * gain_vec.astype(F32) + bias_vec.astype(F32), normed, inv_std)


def norm_back(grad_out, normed, inv_std, gain_vec):
    scaled = grad_out * gain_vec.astype(F32)
    inner = (
        scaled
        - jnp.mean(scaled, axis=-1, keepdims=True)
        - normed * jnp.mean(scaled * normed, axis=-1, keepdims=True)
    )
    return (inv_std * inner, jnp.sum(grad_out * normed, axis=0), jnp.sum(grad_out, axis=0))


def rotary_tables(segment_row):
    count_tok = segment_row.shape[0]
    earlier = jnp.sum((segment_row[None, :] < segment_row[:, None]).astype(jnp.int32), axis=1)
    places = (jnp.arange(count_tok, dtype=jnp.int32) - earlier).astype(F32)
    frequency = jnp.exp(jnp.arange(ROT // 2, dtype=F32) * (-2.0 * THETA_LOG / ROT))
    angles = places[:, None] * frequency[None, :]
    cosine, sine = jnp.cos(angles), jnp.sin(angles)
    rest = HD - ROT
    half = jnp.zeros((count_tok, ROT // 2), F32)
    none = jnp.zeros((count_tok, rest), F32)
    cos_head = jnp.concatenate([cosine, cosine, none + 1.0], axis=1)
    first_head = jnp.concatenate([-sine, half, none], axis=1)
    second_head = jnp.concatenate([half, sine, none], axis=1)
    return tuple(jnp.tile(t, (1, HEADS_STEP)) for t in (cos_head, first_head, second_head))


def mul_rows(left, weight):
    return lax.dot_general(left, weight, (((1,), (1,)), ((), ())), preferred_element_type=F32)


def weight_grad(grad_rows, inputs):
    return lax.dot_general(grad_rows, inputs, (((0,), (0,)), ((), ())), preferred_element_type=F32)


def shifts(field):
    half = ROT // 2
    return (pltpu.roll(field, LANES - half, 1), pltpu.roll(field, half, 1))


def lane_masks(scale):
    head_of = lax.broadcasted_iota(jnp.int32, (1, LANES), 1) // HD
    return [jnp.where(head_of == head, scale, 0.0).astype(BF) for head in range(HEADS_STEP)]


def by_head(rows, masks):
    return jnp.concatenate([rows * mask for mask in masks], axis=0)


def joined(field, masks):
    parts = jnp.split(field, HEADS_STEP, axis=0)
    return sum(part * mask.astype(F32) for part, mask in zip(parts, masks))


def probs_of(queries, keys, allowed):
    scores = jnp.where(allowed, mul_rows(keys, queries), NEG_FILL)
    unnormed = jnp.exp(scores - jnp.max(scores, axis=0, keepdims=True))
    return unnormed * (1.0 / jnp.sum(unnormed, axis=0, keepdims=True))


def allowed_of(seg_col, seg_row, block):
    start, end = block * Q_BLOCK, (block + 1) * Q_BLOCK
    key_at = lax.broadcasted_iota(jnp.int32, (end, Q_BLOCK), 0)
    query_at = lax.broadcasted_iota(jnp.int32, (end, Q_BLOCK), 1) + start
    one = (seg_col[:end, :] == seg_row[:, start:end]) & (key_at <= query_at)
    return jnp.concatenate([one] * HEADS_STEP, axis=1)


def attend_kernel(
    x_ref, wq_ref, wk_ref, wv_ref, bq_ref, bk_ref, bv_ref, cos_ref, first_ref, second_ref,
    segc_ref, segr_ref, q_ref, k_ref, v_ref, out_ref,
):
    x_in = x_ref[...]
    cosine, first, second = cos_ref[...], first_ref[...], second_ref[...]

    def turned(w_ref, b_ref):
        field = mul_rows(x_in, w_ref[...]) + b_ref[...]
        ahead, behind = shifts(field)
        return (field * cosine + ahead * first + behind * second).astype(BF)

    q_ref[...] = turned(wq_ref, bq_ref)
    k_ref[...] = turned(wk_ref, bk_ref)
    v_ref[...] = (mul_rows(x_in, wv_ref[...]) + bv_ref[...]).astype(BF)
    scaled, masks = lane_masks(1.0 / math.sqrt(HD)), lane_masks(1.0)
    seg_col, seg_row = segc_ref[...], segr_ref[...]
    for block in range(x_in.shape[0] // Q_BLOCK):
        start, end = block * Q_BLOCK, (block + 1) * Q_BLOCK
        queries = by_head(q_ref[start:end, :], scaled)
        probs = probs_of(queries, k_ref[:end, :], allowed_of(seg_col, seg_row, block))
        out_ref[start:end, :] = joined(weight_grad(probs.astype(BF), v_ref[:end, :]), masks).astype(BF)


def attend_back_kernel(
    q_ref, k_ref, v_ref, g_ref, cos_ref, first_ref, second_ref, segc_ref, segr_ref, *rest
):
    grad_ref, dk_sum, dv_sum = rest[-3:]
    cosine, first, second = cos_ref[...], first_ref[...], second_ref[...]
    scale = 1.0 / math.sqrt(HD)
    width = grad_ref.shape[1] // 3

    def columns(which):
        return pl.ds(pl.multiple_of(which * width + pl.program_id(1) * LANES, LANES), LANES)

    def turned_back(field, start, end):
        ahead, behind = shifts(field)
        turned = field * cosine[start:end] - ahead * first[start:end] - behind * second[start:end]
        return turned.astype(BF)

    dk_sum[...] = jnp.zeros_like(dk_sum)
    dv_sum[...] = jnp.zeros_like(dv_sum)
    scaled, masks = lane_masks(scale), lane_masks(1.0)
    seg_col, seg_row = segc_ref[...], segr_ref[...]
    for block in range(q_ref.shape[0] // Q_BLOCK):
        start, end = block * Q_BLOCK, (block + 1) * Q_BLOCK
        keys, values = k_ref[:end, :], v_ref[:end, :]
        queries = by_head(q_ref[start:end, :], scaled)
        grads = by_head(g_ref[start:end, :], masks)
        probs = probs_of(queries, keys, allowed_of(seg_col, seg_row, block))
        grad_probs = mul_rows(values, grads)
        dots = jnp.sum(probs * grad_probs, axis=0, keepdims=True)
        grad_scores = (probs * (grad_probs - dots)).astype(BF)
        dv_sum[:end, :] += jnp.dot(probs.astype(BF), grads, preferred_element_type=F32)
        dk_sum[:end, :] += jnp.dot(grad_scores, queries, preferred_element_type=F32)
        dq_rows = joined(weight_grad(grad_scores, keys), masks) * scale
        grad_ref[start:end, columns(0)] = turned_back(dq_rows, start, end)
    grad_ref[:, columns(1)] = turned_back(dk_sum[...], 0, dk_sum.shape[0])
    grad_ref[:, columns(2)] = dv_sum[...].astype(BF)


def of_sequence(shape):
    return pl.BlockSpec(shape, lambda step, seq: (seq, 0))


def row_of_sequence(count_tok):
    return pl.BlockSpec((None, 1, count_tok), lambda step, seq: (seq, 0, 0))


def attend(normed_in, weight, bias_row, tables, seg_col, seg_row):
    count_tok = seg_row.shape[2]
    rows, cols = normed_in.shape[0], weight.shape[0] // 3
    steps = cols // LANES
    head_cols = pl.BlockSpec((count_tok, LANES), lambda step, seq: (seq, step))

    def part(which):
        return pl.BlockSpec((LANES, D), lambda step, seq: (which * steps + step, 0))

    def bias_part(which):
        return pl.BlockSpec((1, LANES), lambda step, seq: (0, which * steps + step))

    return pl.pallas_call(
        attend_kernel,
        grid=(steps, rows // count_tok),
        in_specs=[of_sequence((count_tok, D))]
        + [part(i) for i in range(3)]
        + [bias_part(i) for i in range(3)]
        + [of_sequence((count_tok, LANES))] * 3
        + [of_sequence((count_tok, 1)), row_of_sequence(count_tok)],
        out_specs=[head_cols] * 4,
        out_shape=[jax.ShapeDtypeStruct((rows, cols), BF)] * 4,
        compiler_params=pltpu.CompilerParams(vmem_limit_bytes=48 << 20),
        cost_estimate=SHORT,
        name="attend",
    )(normed_in, weight, weight, weight, bias_row, bias_row, bias_row, *tables, seg_col, seg_row)


def attend_back(query, key_rot, value_in, grad_attended, tables, seg_col, seg_row, first_seq, others):
    count_tok = seg_row.shape[2]
    rows, cols = grad_attended.shape

    def of_heads(first):
        return pl.BlockSpec((count_tok, LANES), lambda seq, step: (seq + first, step))

    def of_seq(shape):
        return pl.BlockSpec(shape, lambda seq, step: (seq + first_seq, 0))

    operands = [query, key_rot, value_in, grad_attended, *tables, seg_col, seg_row]
    in_specs = (
        [of_heads(first_seq)] * 3
        + [of_heads(0)]
        + [of_seq((count_tok, LANES))] * 3
        + [of_seq((count_tok, 1))]
        + [pl.BlockSpec((None, 1, count_tok), lambda seq, step: (seq + first_seq, 0, 0))]
    )
    aliases = {}
    if others is not None:
        aliases = {len(operands): 0}
        operands.append(others)
        in_specs.append(pl.BlockSpec(memory_space=pl.ANY))
    return pl.pallas_call(
        attend_back_kernel,
        grid=(rows // count_tok, cols // LANES),
        in_specs=in_specs,
        out_specs=of_seq((count_tok, 3 * cols)),
        out_shape=jax.ShapeDtypeStruct((query.shape[0], 3 * cols), BF),
        scratch_shapes=[pltpu.VMEM((count_tok, LANES), F32)] * 2,
        input_output_aliases=aliases,
        compiler_params=pltpu.CompilerParams(vmem_limit_bytes=48 << 20),
        cost_estimate=SHORT,
        name="attend_back",
    )(*operands)


def rows_product(left, right, first_row, count_rows, right_rows=False):
    inner, cols = right.shape[::-1] if right_rows else right.shape
    width = 512

    def kernel(left_ref, right_ref, out_ref):
        if right_rows:
            out_ref[...] = mul_rows(left_ref[...], right_ref[...])
        else:
            out_ref[...] = jnp.dot(left_ref[...], right_ref[...], preferred_element_type=F32)

    if right_rows:
        right_spec = pl.BlockSpec((width, inner), lambda n: (n, 0))
    else:
        right_spec = pl.BlockSpec((inner, width), lambda n: (0, n))
    return pl.pallas_call(
        kernel,
        grid=(cols // width,),
        in_specs=[
            pl.BlockSpec((count_rows, inner), lambda n: (first_row // count_rows, 0)),
            right_spec,
        ],
        out_specs=pl.BlockSpec((count_rows, width), lambda n: (0, n)),
        out_shape=jax.ShapeDtypeStruct((count_rows, cols), F32),
        compiler_params=pltpu.CompilerParams(vmem_limit_bytes=48 << 20),
        cost_estimate=SHORT,
        name="rows_product",
    )(left, right)


def attention_grads(half, side_at, grad_proj, inputs, grad_attn, attended, line, group):
    count_rows, proj_cols = grad_proj.shape
    cols = attended.shape[1]
    qkv_rows, out_rows = proj_cols // (2 * line), D // (2 * line)
    share = out_rows // group
    width = D // 2
    members = width // cols
    rows = qkv_rows + share
    pair_rows = grad_attn[0].shape[0]

    def kernel(side_ref, proj_ref, input_ref, attended_ref, *refs):
        attn_refs, (away_ref, mine_ref) = refs[:-2], refs[-2:]
        qkv = weight_grad(proj_ref[...], input_ref[...])
        blocks = []
        for side in range(2):
            start = side * out_rows + half * (members * share)
            out = sum(
                weight_grad(
                    attn_ref[:, start : start + members * share],
                    attended_ref[pair * pair_rows : (pair + 1) * pair_rows, :],
                )
                for pair, attn_ref in enumerate(attn_refs)
            )
            out = jnp.concatenate([out[m * share : (m + 1) * share] for m in range(members)], axis=1)
            blocks.append((qkv[side * qkv_rows : (side + 1) * qkv_rows], out))

        def store(mine, away):
            mine_ref[:qkv_rows, :] = blocks[mine][0]
            mine_ref[qkv_rows:, :] = blocks[mine][1]
            away_ref[:qkv_rows, :] = blocks[away][0].astype(BF)
            away_ref[qkv_rows:, :] = blocks[away][1].astype(BF)

        pl.when(side_ref[0] == 0)(lambda: store(0, 1))
        pl.when(side_ref[0] != 0)(lambda: store(1, 0))

    out_block = pl.BlockSpec((None, rows, width), lambda z, side: (z, 0, 0))
    return pl.pallas_call(
        kernel,
        grid_spec=pltpu.PrefetchScalarGridSpec(
            num_scalar_prefetch=1,
            grid=(line,),
            in_specs=[
                pl.BlockSpec((count_rows, 2 * qkv_rows), lambda z, side: (0, z)),
                pl.BlockSpec((count_rows, width), lambda z, side: (0, half)),
                pl.BlockSpec((count_rows, cols), lambda z, side: (0, 0)),
            ]
            + [pl.BlockSpec((pair_rows, 2 * out_rows), lambda z, side: (0, z))] * len(grad_attn),
            out_specs=[out_block, out_block],
        ),
        out_shape=[
            jax.ShapeDtypeStruct((line, rows, width), BF),
            jax.ShapeDtypeStruct((line, rows, width), F32),
        ],
        compiler_params=pltpu.CompilerParams(vmem_limit_bytes=56 << 20),
        cost_estimate=SHORT,
        name="attention_grads",
    )(side_at.reshape(1), grad_proj, inputs, attended, *grad_attn)


class Layout:
    def __init__(self, n_wide, n_narrow):
        self.narrow = n_narrow
        self.count = n_wide * n_narrow
        self.group = 2 * n_narrow
        self.outer = n_wide // 2
        self.line = self.outer // 2
        self.core_mask = n_narrow
        self.side_mask = 2 * n_narrow
        self.line_mask = 4 * n_narrow
        self.shifts = list(range(1, n_narrow))
        self.outer_groups = [
            [o * self.group + member for o in range(self.outer)] for member in range(self.group)
        ]

    def swap(self, value, mask):
        return lax.ppermute(value, AXES, [(i, i ^ mask) for i in range(self.count)])


    def gather_pairs(self, value, meanwhile=None):
        own = (value, self.swap(value, self.core_mask))
        shifted = [self.swap(value, mask) for mask in self.shifts]
        done = None
        if meanwhile is not None:
            shifted, done = lax.optimization_barrier((shifted, meanwhile(own)))
        return [own] + [(block, self.swap(block, self.core_mask)) for block in shifted], done

    def across_cores(self, partials):
        summed = []
        for partial in partials:
            own, sent = jnp.split(partial, 2)
            summed.append(own + self.swap(sent.astype(BF), self.core_mask).astype(F32))
        return summed

    def across_shifts(self, summed, meanwhile=None):
        shifted = [self.swap(part.astype(BF), mask) for part, mask in zip(summed[1:], self.shifts)]
        if meanwhile is not None:
            shifted, meanwhile = lax.optimization_barrier((shifted, meanwhile))
        return sum((part.astype(F32) for part in shifted), start=summed[0]), meanwhile

    def swap_group(self, pieces, member):
        result = jnp.zeros(pieces.shape, pieces.dtype)
        for mask in range(self.group):
            piece = lax.dynamic_index_in_dim(pieces, member ^ mask, 0, keepdims=False)
            if mask:
                piece = self.swap(piece, mask)
            result = lax.dynamic_update_index_in_dim(result, piece, member ^ mask, 0)
        return result


    def gather_outer(self, value):
        return lax.all_gather(value, AXES, axis=0, axis_index_groups=self.outer_groups)

    def scatter_outer(self, value):
        return lax.psum_scatter(
            value, AXES, scatter_dimension=0, tiled=True, axis_index_groups=self.outer_groups
        )

    def by_side(self, grad, place):
        by_place = grad.reshape(self.line, 2, -1, grad.shape[1])
        away = lax.dynamic_index_in_dim(by_place, 1 - place % 2, 1, keepdims=False).astype(BF)
        return away, lax.dynamic_index_in_dim(by_place, place % 2, 1, keepdims=False)

    def across_sides(self, away, mine):
        return mine + self.swap(away, self.side_mask).astype(F32)

    def line_steps(self):
        return [1 << bit for bit in range(self.line.bit_length() - 1)]

    def along_line(self, mine, place, step):
        pairs = mine.reshape(-1, 2, *mine.shape[1:])
        at = place // 2 // step % 2
        away = lax.dynamic_index_in_dim(pairs, 1 - at, 1, keepdims=False).astype(BF)
        mine = lax.dynamic_index_in_dim(pairs, at, 1, keepdims=False)
        return mine + self.swap(away, step * self.line_mask).astype(F32)


    def gather_small(self, row, index):
        blocks = row
        mask = 1
        while mask < self.line_mask:
            blocks = jnp.concatenate([blocks, self.swap(blocks, mask)])
            mask *= 2
        blocks = jnp.concatenate(
            [blocks] + [self.swap(blocks, step * self.line_mask) for step in range(1, self.line)]
        )
        return jnp.dot(self.by_mask(index).astype(row.dtype), blocks, preferred_element_type=F32)

    def scatter_small_line(self, rows, index):
        rows = jnp.dot(self.by_mask(index).astype(F32), rows, precision=lax.Precision.HIGHEST)
        blocks = jnp.split(rows, self.line)
        total = blocks[0]
        for step in range(1, self.line):
            total = total + self.swap(blocks[step], step * self.line_mask)
        return total

    def scatter_small_rest(self, total):
        mask = self.side_mask
        while mask:
            total = total[:mask] + self.swap(total[mask:], mask)
            mask //= 2
        return total

    def by_mask(self, index):
        numbers = jnp.arange(self.count, dtype=jnp.int32)
        return (numbers[:, None] ^ numbers[None, :]) == index


def deal_heads(layout, weight, member):
    per, group = weight.shape[0] // HD, layout.group
    got = [
        lax.ppermute(
            block,
            AXES,
            [(i, i // group * group + (per * i + j) % group) for i in range(layout.count)],
        )
        for j, block in enumerate(jnp.split(weight, per))
    ]
    stacked = jnp.stack(got)
    order = [lax.rem(k * group + member, per) for k in range(per)]
    return jnp.concatenate(
        [lax.dynamic_index_in_dim(stacked, j, 0, keepdims=False) for j in order]
    )


def deal_back(layout, rows, member):
    per, group = rows.shape[0] // HD, layout.group
    blocks = rows.reshape(per, HD, rows.shape[1])
    result = []
    for j in range(per):
        chosen = blocks[0]
        for k in range(1, per):
            chosen = jnp.where(lax.rem(k * group + member, per) == j, blocks[k], chosen)
        pairs = [(i // group * group + (per * i + j) % group, i) for i in range(layout.count)]
        result.append(lax.ppermute(chosen, AXES, pairs))
    return jnp.concatenate(result)


def heads_dealt(layout, qkv_rows):
    return qkv_rows % HD == 0 and math.gcd(qkv_rows // HD, layout.group) == 1


def gather_attention(layout, qkv_weight, out_weight, member):
    qkv_rows, share = qkv_weight.shape[0], out_weight.shape[0]
    cols = D // layout.group
    out_pieces = jnp.transpose(
        out_weight.reshape(share, H // layout.group, layout.group, HD), (2, 0, 1, 3)
    ).reshape(layout.group, share, cols)
    out_mine = layout.swap_group(out_pieces, member)
    out_mine = out_mine.reshape(layout.group * share, cols)
    if not heads_dealt(layout, qkv_rows):
        full = lax.all_gather(qkv_weight, AXES, axis=0, tiled=True)
        split = full.reshape(3 * H // layout.group, layout.group, HD, D)
        mine = lax.dynamic_index_in_dim(split, member, 1, keepdims=False).reshape(-1, D)
        return mine, layout.gather_outer(out_mine).reshape(D, cols)
    both = jnp.concatenate([deal_heads(layout, qkv_weight, member), out_mine.reshape(share, D)])
    full = layout.gather_outer(both)
    return full[:, :qkv_rows].reshape(-1, D), full[:, qkv_rows:].reshape(D, cols)


def scatter_attention(layout, grad_proj, inputs, grad_attn, attended, qkv_rows, place, first, second):
    steps = layout.line_steps()
    if not heads_dealt(layout, qkv_rows):
        group = layout.group
        split = jnp.zeros((3 * H // group, group, HD, D), BF)
        grad = weight_grad(grad_proj, inputs).astype(BF).reshape(-1, 1, HD, D)
        split = lax.dynamic_update_index_in_dim(split, grad, lax.axis_index(AXES) % group, 1)
        qkv_sum = lax.psum_scatter(split.reshape(-1, D), AXES, scatter_dimension=0, tiled=True)
        out_own = weight_grad(jnp.concatenate(grad_attn), attended)
        out_sum = layout.across_sides(*layout.by_side(out_own, place))
        for step in steps:
            out_sum = layout.along_line(out_sum, place, step)
        return qkv_sum, out_sum[0].astype(BF), second(first(grad_proj))
    others = (inputs, grad_attn, attended, layout.line, layout.group)
    away, mine = attention_grads(0, place % 2, grad_proj, *others)
    away, mine, grad_proj = lax.optimization_barrier((away, mine, grad_proj))
    left = layout.across_sides(away, mine)
    away, mine = attention_grads(1, place % 2, grad_proj, *others)
    left, away, mine, done = lax.optimization_barrier((left, away, mine, first(grad_proj)))
    left = layout.along_line(left, place, steps[0])
    right = layout.across_sides(away, mine)
    left, right, done = lax.optimization_barrier((left, right, second(done)))
    for step in steps[1:]:
        left = layout.along_line(left, place, step)
    right = layout.along_line(right, place, steps[0])
    left, right, last = lax.optimization_barrier((left, right, done[0]))
    done = (last, *done[1:])
    for step in steps[1:]:
        right = layout.along_line(right, place, step)
    summed = jnp.concatenate([left[0].astype(BF), right[0].astype(BF)], axis=1)
    out_sum = summed[qkv_rows:].reshape(-1, layout.group, D // layout.group)
    return summed[:qkv_rows], jnp.transpose(out_sum, (1, 0, 2)).reshape(-1, D // layout.group), done


def per_device(
    layout,
    tokens,
    segment_ids,
    language_ids,
    lang_table,
    norm1_gain,
    norm1_bias,
    qkv_weight,
    qkv_bias,
    out_weight,
    norm2_gain,
    norm2_bias,
    gate_up_weight,
    down_weight,
    cotangent,
):
    count_tok = tokens.shape[0]
    group, outer, count, narrow = layout.group, layout.outer, layout.count, layout.narrow
    index = lax.axis_index(AXES)
    member, place = lax.rem(index, group), index // group
    share = D // count
    unit_rows = gate_up_weight.shape[0]
    units = FF // group
    head_cols = D // group

    small = jnp.concatenate(
        [
            lang_table.T,
            norm1_gain[None],
            norm1_bias[None],
            norm2_gain[None],
            norm2_bias[None],
            qkv_bias.reshape(3, share),
        ]
    )
    small_len = SMALL_ROWS * share
    small_all = layout.gather_small(small.reshape(1, small_len), index)
    small_all = small_all.reshape(count, SMALL_ROWS, share)
    small_rows = jnp.transpose(small_all, (1, 0, 2)).reshape(SMALL_ROWS, D)
    table_rows = small_rows[:LANGS].astype(BF)
    gain1, bias1, gain2, bias2 = (small_rows[LANGS + i] for i in range(4))
    bias_heads = small_all[:, LANGS + 4 :].reshape(3, H // group, group, HD)
    bias_row = lax.dynamic_index_in_dim(bias_heads, member, 2, keepdims=False).reshape(
        1, 3 * head_cols
    )

    qkv_part, out_part = gather_attention(layout, qkv_weight, out_weight, member)
    gate_up_part = layout.gather_outer(gate_up_weight).reshape(2 * units, D)
    down_pieces = jnp.transpose(
        down_weight.reshape(share, outer // 2, group, unit_rows), (2, 0, 1, 3)
    ).reshape(group, share, units)
    down_mine = layout.swap_group(down_pieces, member).reshape(group * share, units)

    segment_pairs, _ = layout.gather_pairs(segment_ids)
    segment_rows = [row for pair in segment_pairs for row in pair]
    seg_row = jnp.stack(segment_rows)
    seg_col = seg_row.reshape(group * count_tok, 1)
    tables = tuple(
        jnp.concatenate(parts) for parts in zip(*(rotary_tables(row[0]) for row in segment_rows))
    )
    one_hot = language_ids[0][:, None] == jnp.arange(LANGS, dtype=jnp.int32)[None, :]
    stream0 = tokens.astype(F32) + jnp.dot(
        one_hot.astype(BF), table_rows, preferred_element_type=F32
    )
    normed_in, norm1_hat, norm1_inv = layer_norm(stream0, gain1, bias1)
    in_pairs, _ = layout.gather_pairs(normed_in.astype(BF))
    in_group = jnp.concatenate(sum(in_pairs, ()))
    in_group, cotangent_late, down_mine = lax.optimization_barrier((in_group, cotangent, down_mine))
    down_part = layout.gather_outer(down_mine).reshape(D, units)
    cot_pairs, _ = layout.gather_pairs(cotangent_late)
    cot_group = jnp.concatenate(sum(cot_pairs, ()))
    query, key_rot, value_in, attended = attend(
        in_group, qkv_part, bias_row, tables, seg_col, seg_row
    )
    attended, cot_group = lax.optimization_barrier((attended, cot_group))
    pair_rows = 2 * count_tok

    def pair_of(value, pair):
        return value[pair * pair_rows : (pair + 1) * pair_rows]

    out_sums = layout.across_cores(
        [mul_rows(pair_of(attended, pair), out_part) for pair in range(narrow)]
    )
    stream1 = stream0 + layout.across_shifts(out_sums)[0]

    normed_mid, norm2_hat, norm2_inv = layer_norm(stream1, gain2, bias2)
    mid_pairs, _ = layout.gather_pairs(normed_mid.astype(BF))
    mid_group = jnp.concatenate(sum(mid_pairs, ()))
    gate_up = mul_rows(mid_group, gate_up_part)
    gate_part, up_part = gate_up[:, :units], gate_up[:, units:]
    sigma_gate = jax.nn.sigmoid(gate_part)
    silu_gate = gate_part * sigma_gate
    hidden = (silu_gate * up_part).astype(BF)
    down_own = weight_grad(cot_group, hidden).astype(BF)
    down_part, down_own = lax.optimization_barrier((down_part, down_own))
    down_sum = layout.scatter_outer(down_own)
    grad_hidden = jnp.dot(cot_group, down_part, preferred_element_type=F32)
    grad_gate = grad_hidden * up_part * (sigma_gate + gate_part * sigma_gate * (1.0 - sigma_gate))
    grad_gu = jnp.concatenate([grad_gate, grad_hidden * silu_gate], axis=1).astype(BF)
    mid_parts = {}
    for pair in reversed(range(narrow)):
        grad_rows = pair_of(grad_gu, pair)
        if pair + 1 in mid_parts:
            grad_rows, mid_parts[pair + 1] = lax.optimization_barrier((grad_rows, mid_parts[pair + 1]))
        mid_parts[pair] = jnp.dot(grad_rows, gate_up_part, preferred_element_type=F32)
    mid_sums = layout.across_cores([mid_parts[pair] for pair in range(narrow)])
    gate_up_own = weight_grad(grad_gu, mid_group).astype(BF)
    grad_mid, gate_up_own = layout.across_shifts(mid_sums, gate_up_own)
    gate_up_sum = layout.scatter_outer(gate_up_own)

    grad_norm2, gain2_grad, bias2_grad = norm_back(grad_mid, norm2_hat, norm2_inv, gain2)
    grad_stream1 = cotangent.astype(F32) + grad_norm2

    def back_of(pair, first_seq, others):
        grad_rows = jnp.concatenate(pair)
        grad_attended = jnp.dot(grad_rows, out_part, preferred_element_type=F32).astype(BF)
        grads = attend_back(
            query, key_rot, value_in, grad_attended, tables, seg_col, seg_row, first_seq, others
        )
        return grads, grad_rows

    def in_the_meantime(pair):
        return back_of(pair, 0, None)

    attn_pairs, (grad_proj, own_rows) = layout.gather_pairs(
        grad_stream1.astype(BF), in_the_meantime
    )
    grad_attn = [own_rows]
    for pair in range(1, narrow):
        grad_proj, grad_rows = back_of(attn_pairs[pair], 2 * pair, grad_proj)
        grad_attn.append(grad_rows)

    def input_grad(grad_proj):
        parts = [
            rows_product(grad_proj, qkv_part, pair * pair_rows, pair_rows) for pair in range(narrow)
        ]
        return layout.across_shifts(layout.across_cores(parts))[0], hidden

    def first_norm(grad_in):
        grad_norm1, gain1_grad, bias1_grad = norm_back(grad_in, norm1_hat, norm1_inv, gain1)
        grad_stream0 = grad_stream1 + grad_norm1
        lang_grad = lax.dot_general(
            one_hot.astype(F32),
            grad_stream0,
            (((0,), (0,)), ((), ())),
            precision=lax.Precision.HIGHEST,
        )
        bias_grad = jnp.zeros((3 * H // group, group, HD), F32)
        bias_grad = lax.dynamic_update_index_in_dim(
            bias_grad, jnp.sum(grad_proj.astype(F32), axis=0).reshape(-1, 1, HD), member, 1
        )
        rows = jnp.concatenate(
            [lang_grad, jnp.stack([gain1_grad, bias1_grad, gain2_grad, bias2_grad])]
        ).reshape(LANGS + 4, count, share)
        small_grad = jnp.concatenate(
            [jnp.transpose(rows, (1, 0, 2)), bias_grad.reshape(count, 3, share)], axis=1
        ).reshape(count, small_len)
        return grad_stream0.astype(BF), small_grad

    def meanwhile(done):
        grad_in, hidden = done
        token_grad, small_grad = first_norm(grad_in)
        small_line = layout.scatter_small_line(small_grad, index)
        mixed_parts = [
            rows_product(hidden, down_part, pair * pair_rows, pair_rows, right_rows=True)
            for pair in range(narrow)
        ]
        down_got = layout.swap_group(down_sum.reshape(group, share, units), member)
        down_grad = jnp.transpose(
            down_got.reshape(group, share, outer // 2, unit_rows), (1, 2, 0, 3)
        ).reshape(share, FF)
        return small_line, token_grad, mixed_parts, gate_up_sum, down_grad

    qkv_sum, out_sum, (small_line, token_grad, mixed_parts, gate_up_sum, down_grad) = scatter_attention(
        layout, grad_proj, in_group, grad_attn, attended, qkv_weight.shape[0], place, input_grad, meanwhile
    )
    mixed_sums = layout.across_cores(mixed_parts)
    small_sum = layout.scatter_small_rest(small_line).reshape(SMALL_ROWS, share)
    mixed = (stream1 + layout.across_shifts(mixed_sums)[0]).astype(BF)

    if heads_dealt(layout, qkv_weight.shape[0]):
        qkv_sum = deal_back(layout, qkv_sum, member)
    out_got = layout.swap_group(out_sum.reshape(group, share, head_cols), member)
    out_grad = jnp.transpose(
        out_got.reshape(group, share, H // group, HD), (1, 2, 0, 3)
    ).reshape(share, D)
    return (
        mixed,
        token_grad,
        small_sum[:LANGS].T,
        small_sum[LANGS],
        small_sum[LANGS + 1],
        qkv_sum.astype(F32),
        small_sum[LANGS + 4 :].reshape(3 * share),
        out_grad.astype(F32),
        small_sum[LANGS + 2],
        small_sum[LANGS + 3],
        gate_up_sum.astype(F32),
        down_grad.astype(F32),
    )


def solution(mesh):
    rows, vector = P(AXES, None), P(AXES)
    layout = Layout(mesh.shape["wide"], mesh.shape["narrow"])
    return jax.shard_map(
        functools.partial(per_device, layout),
        mesh=mesh,
        in_specs=(rows, rows, rows, rows, vector, vector, rows, vector, rows, vector, vector, rows, rows, rows),
        out_specs=(rows, rows, rows, vector, vector, rows, vector, rows, vector, vector, rows, rows),
        check_vma=False,
    )
```
